768 devices in a mesh: blk: 48 (over z, x), rep: 16 (over y, core).
Axes of the slice: x: 4, y: 8, z: 12, core: 2. Of those that a mesh axis runs over, the one named last changes fastest.
Arguments:
- image_feats: bfloat16 [98304, 1152], P(('blk', 'rep')), may hold values from -6 to 6
- head_weight: bfloat16 [1152, 1152], replicated, may hold values from -0.1875 to 0.1875
- text_embeds: bfloat16 [98304, 1152], P(('blk', 'rep')), may hold values from -6 to 6
- positives: int32 [48, 2048], P('blk', 'rep'), may hold values from 0 to 2047, each once within a row
- logit_scale: float32 [1], replicated, may hold values from 20 to 40
- logit_bias: float32 [1], replicated, may hold values from -7 to -5
- loss_scale: float32 [1], replicated, may hold values from 16 to 64
Outputs:
- image_grads: bfloat16 [98304, 1152], P(('blk', 'rep'))
- text_grads: bfloat16 [98304, 1152], P(('blk', 'rep'))
- head_grad: float32 [48, 1152, 1152], P('blk', 'rep')
The draws below stay inside these ranges and needn't reach their ends.
Inputs may be any that keep to these rules, and one draw needn't show every extreme that they name: Each row of positives names every position of a block once.
All inputs are finite; a program needn't handle non-finite values.
Results may differ from the reference program's by a relative error of at most 0.034.
Values may be sent and summed in bfloat16 or wider, within the bound.
No kernel may reach another device: no remote copies, remote signals or barrier semaphores. Data moves between devices by JAX's collectives and lax.ppermute only.
A program may use at most 64 MiB of HBM per device.

```python
import math
import jax
import jax.numpy as jnp
from jax import lax

D = 1152
ROWS_DEV = 128
STEPS = 3
BLOCKS = 48
BLOCK = 2048
IMAGES = 98304
N_REP = 16


def block_levels(rng, dims, shards, smallest, top_value):
    def one(position, blocks):
        steps = jax.random.uniform(jax.random.fold_in(jax.random.fold_in(rng, 6), position), (blocks,), jnp.float32, smallest / len(shards), top_value / len(shards))
        return jnp.repeat(jnp.exp(steps), dims[position] // blocks).reshape((-1,) + (1,) * (len(dims) - position - 1))

    gain = one(*shards[0])
    for cut in shards[1:]:
        gain = gain * one(*cut)
    return gain


def normal_values(stream_key, dims, deviation, reach, split=(), kind=jnp.bfloat16):
    values = deviation * jax.random.normal(stream_key, dims, jnp.float32)
    if split:
        values = values * block_levels(stream_key, dims, split, -0.22, 0.18)
    return jnp.clip(values, -reach, reach).astype(kind)


def setup_inputs(seed: int = 0) -> dict:
    streams_of = jax.random.split(jax.random.key(seed), 8)
    return {
        "image_feats": normal_values(streams_of[0], (IMAGES, D), 1.0, 6.0, ((0, 768),)),
        "head_weight": normal_values(streams_of[1], (D, D), D ** -0.5, 0.1875),
        "text_embeds": normal_values(streams_of[2], (IMAGES, D), 1.0, 6.0, ((0, 768),)),
        "positives": jax.vmap(lambda own: jax.random.permutation(own, BLOCK))(jax.random.split(streams_of[3], BLOCKS)).reshape((BLOCKS, BLOCK)).astype(jnp.int32),
        "logit_scale": jnp.clip(jax.random.uniform(streams_of[4], (1,), jnp.float32, 20.0, 40.0), 20.0, 40.0),
        "logit_bias": jnp.clip(jax.random.uniform(streams_of[5], (1,), jnp.float32, -7.0, -5.0), -7.0, -5.0),
        "loss_scale": jnp.clip(jnp.exp(jax.random.uniform(streams_of[6], (1,), jnp.float32, math.log(16.0), math.log(64.0))), 16.0, 64.0),
    }


EPSILON = 1e-06

def normalize(vectors):
    return vectors * lax.rsqrt(lax.optimization_barrier(jnp.mean(vectors * vectors, axis=-1, keepdims=True)) + EPSILON) / math.sqrt(vectors.shape[-1])

def rounded(values):
    return lax.optimization_barrier(values.astype(jnp.bfloat16)).astype(jnp.float32)

def reference(image_feats, head_weight, text_embeds, positives, logit_scale, logit_bias, loss_scale):
    hidden = jnp.dot(image_feats, head_weight, preferred_element_type=jnp.float32)
    image_unit, image_pull = jax.vjp(normalize, hidden)
    text_unit, text_pull = jax.vjp(normalize, text_embeds.astype(jnp.float32))
    image_blocks = rounded(image_unit).reshape(BLOCKS, BLOCK, D)
    text_blocks = rounded(text_unit).reshape(BLOCKS, BLOCK, D)
    temper = logit_scale[0]
    offset_bias = logit_bias[0]
    weighting = loss_scale[0] * temper
    places = jnp.arange(BLOCK, dtype=jnp.int32)
    block_ids = jnp.arange(BLOCKS, dtype=jnp.int32)

    def coefficients(logits, labels):
        return rounded(weighting * -labels * jax.nn.sigmoid(-labels * logits))

    def image_side(index):
        images = image_blocks[index]
        accum = jnp.zeros((N_REP, BLOCK, D), jnp.float32)
        for offset in range(STEPS):
            texts = text_blocks[(index - offset) % BLOCKS].reshape(N_REP, ROWS_DEV, D)
            logits = temper * jnp.einsum('pd,rcd->rpc', images, texts) + offset_bias
            if offset == 0:
                matches = positives[index][:, None] == places[None, :]
                labels = jnp.where(matches, 1.0, -1.0).astype(jnp.float32).reshape(BLOCK, N_REP, ROWS_DEV).transpose(1, 0, 2)
            else:
                labels = -jnp.ones_like(logits)
            accum = accum + jnp.einsum('rpc,rcd->rpd', coefficients(logits, labels), texts)
        return lax.optimization_barrier(jnp.sum(rounded(accum), axis=0))

    def text_side(index):
        texts = text_blocks[index]
        accum = jnp.zeros((BLOCK, D), jnp.float32)
        for offset in range(STEPS):
            source = (index + offset) % BLOCKS
            images = image_blocks[source]
            logits = temper * jnp.einsum('pd,cd->pc', images, texts) + offset_bias
            if offset == 0:
                matches = positives[source][:, None] == places[None, :]
                labels = jnp.where(matches, 1.0, -1.0).astype(jnp.float32)
            else:
                labels = -jnp.ones_like(logits)
            accum = accum + jnp.einsum('pc,pd->cd', coefficients(logits, labels), images)
        return accum
    image_total = lax.map(image_side, block_ids)
    text_total = lax.map(text_side, block_ids)
    hidden_grad = image_pull(image_total.reshape(IMAGES, D))[0].astype(jnp.bfloat16)
    image_grads = jnp.dot(hidden_grad, head_weight.T, preferred_element_type=jnp.float32).astype(jnp.bfloat16)
    feats_split = image_feats.reshape(BLOCKS, N_REP, ROWS_DEV, D)
    grads_split = hidden_grad.reshape(BLOCKS, N_REP, ROWS_DEV, D)

    def block_head(pair):
        feats_block, grads_block = pair
        partial_terms = jnp.einsum('rkd,rke->rde', feats_block.astype(jnp.float32), grads_block.astype(jnp.float32), precision=lax.Precision.HIGHEST)
        return lax.optimization_barrier(jnp.sum(rounded(partial_terms), axis=0))
    head_grad = lax.map(block_head, (feats_split, grads_split))
    text_grads = text_pull(text_total.reshape(IMAGES, D))[0].astype(jnp.bfloat16)
    return (image_grads, text_grads, head_grad)
```

```python
import functools
import math

import jax
import jax.numpy as jnp
from jax import lax
from jax.experimental import pallas as pl
from jax.experimental.pallas import tpu as pltpu
from jax.sharding import PartitionSpec as P

STEPS = 3
EPSILON = 1e-06
D = 1152
ROWS = 128
WIDE = 1280
SLICE = 72
VMEM_LIMIT = 48 * 1024 * 1024
ROOT = 1.0 / math.sqrt(D)

ROWS_BY_ROWS = (((1,), (1,)), ((), ()))
DEPTH_FIRST = (((0,), (0,)), ((), ()))


def unit_of(values):
    scale = lax.rsqrt(jnp.mean(values * values, axis=-1, keepdims=True) + EPSILON) * ROOT
    return values * scale, scale


def unit_pull(unit, scale, grad):
    return scale * (grad - unit * jnp.sum(unit * grad, axis=-1, keepdims=True))


def whole(count):
    return [pl.BlockSpec(memory_space=pltpu.VMEM)] * count


def call(kernel, out_shape, operands, scalars, flops, scratch=()):
    moved = sum(math.prod(a.shape) * a.dtype.itemsize for a in list(operands) + list(out_shape))
    return pl.pallas_call(
        kernel,
        out_shape=out_shape,
        in_specs=[pl.BlockSpec(memory_space=pltpu.SMEM)] * len(scalars) + whole(len(operands)),
        out_specs=whole(len(out_shape)),
        scratch_shapes=list(scratch),
        compiler_params=pltpu.CompilerParams(vmem_limit_bytes=VMEM_LIMIT),
        cost_estimate=pl.CostEstimate(flops=flops, bytes_accessed=moved, transcendentals=0),
    )(*scalars, *operands)


def tile_kernel(count, scal, weight, texts, *refs):
    tiles, (part_ref, grad_ref, unit_ref, coeff_ref) = refs[:count], refs[count:]
    temper, offset_bias, weighting, mine, other = (scal[i] for i in range(5))
    feats = jnp.concatenate([t[:, :D] for t in tiles], axis=0) if count > 1 else tiles[0][:, :D]
    digits = [t[:, D:].astype(jnp.float32) for t in tiles]
    place = jnp.concatenate([d[:, 0:1] * 128.0 + d[:, 1:2] for d in digits], axis=0)
    hidden = jnp.dot(feats, weight[...], preferred_element_type=jnp.float32)
    unit, scale = unit_of(hidden)
    low = unit.astype(jnp.bfloat16)
    unit_ref[...] = low
    part = jnp.zeros((count * ROWS, D), jnp.float32)
    for k in range(STEPS):
        text = texts[k * 256 : (k + 1) * 256, :]
        logits = (
            temper * lax.dot_general(low, text, ROWS_BY_ROWS, preferred_element_type=jnp.float32)
            + offset_bias
        )
        if k == 0:
            lane = lax.broadcasted_iota(jnp.int32, (1, 256), 1)
            base = jnp.where(lane < 128, mine, other - 128.0)
            match = place == base + lane.astype(jnp.float32)
            logits = jnp.where(match, -logits, logits)
            weights = jnp.where(match, -weighting, weighting)
        else:
            weights = weighting
        coeffs = (weights / (1.0 + jnp.exp(-logits))).astype(jnp.bfloat16)
        coeff_ref[:, k * 256 : (k + 1) * 256] = coeffs
        part = part + jnp.dot(coeffs, text, preferred_element_type=jnp.float32)
    part_ref[...] = part.astype(jnp.bfloat16)
    grad_ref[...] = unit_pull(unit, scale, part).astype(jnp.bfloat16)


def tile_terms(scal, weight, texts, tiles):
    rows = len(tiles) * ROWS
    shape = lambda width: jax.ShapeDtypeStruct((rows, width), jnp.bfloat16)
    return call(
        functools.partial(tile_kernel, len(tiles)),
        [shape(D), shape(D), shape(D), shape(STEPS * 256)],
        [weight, texts, *tiles],
        [scal],
        2 * rows * D * (D + 2 * STEPS * 256),
    )


def head_kernel(tile_count, grad_count, index, *refs):
    tiles = refs[:tile_count]
    grads = refs[tile_count : tile_count + grad_count]
    mine_ref, other_ref, feats, hidden_grads, total = refs[tile_count + grad_count :]
    for n, tile in enumerate(tiles):
        feats[n * ROWS : (n + 1) * ROWS, :] = tile[:, :D]
    at = 0
    for grad in grads:
        hidden_grads[at : at + grad.shape[0], :] = grad[...]
        at += grad.shape[0]

    def column(n, _):
        start = pl.multiple_of(n * 128, 128)
        total[pl.ds(start, 128), :] = lax.dot_general(
            feats[:, pl.ds(start, 128)], hidden_grads[...], DEPTH_FIRST, preferred_element_type=jnp.float32
        )
        return _

    lax.fori_loop(0, D // 128, column, 0)
    for n in range(8):
        mine_ref[n] = total[pl.ds(pl.multiple_of(index[n] * SLICE, 8), SLICE), :]
        other_ref[n] = total[pl.ds(pl.multiple_of(index[8 + n] * SLICE, 8), SLICE), :].astype(jnp.bfloat16)


def head_terms(index, tiles, grads):
    rows = ROWS * len(tiles)
    return call(
        functools.partial(head_kernel, len(tiles), len(grads)),
        [
            jax.ShapeDtypeStruct((8, SLICE, D), jnp.float32),
            jax.ShapeDtypeStruct((8, SLICE, D), jnp.bfloat16),
        ],
        [*tiles, *grads],
        [index],
        2 * rows * D * D,
        [
            pltpu.VMEM((rows, D), jnp.bfloat16),
            pltpu.VMEM((rows, D), jnp.bfloat16),
            pltpu.VMEM((D, D), jnp.float32),
        ],
    )


def text_kernel(count, *refs):
    coeffs, units, (mine_ref, other_ref) = refs[:count], refs[count : 2 * count], refs[2 * count :]
    for k in range(2 * STEPS):
        total = jnp.zeros((ROWS, D), jnp.float32)
        for coeff, unit in zip(coeffs, units):
            total = total + lax.dot_general(
                coeff[:, k * ROWS : (k + 1) * ROWS], unit[...], DEPTH_FIRST, preferred_element_type=jnp.float32
            )
        if k % 2 == 0:
            mine_ref[k // 2] = total
        else:
            other_ref[k // 2] = total.astype(jnp.bfloat16)


def text_terms(coeffs, units):
    return call(
        functools.partial(text_kernel, len(coeffs)),
        [
            jax.ShapeDtypeStruct((STEPS, ROWS, D), jnp.float32),
            jax.ShapeDtypeStruct((STEPS, ROWS, D), jnp.bfloat16),
        ],
        [*coeffs, *units],
        [],
        2 * 8 * ROWS * 2 * STEPS * ROWS * D,
    )


def ring_maps(chips):
    def dev(y, c):
        return 2 * (y % chips) + c

    out = [(dev(y, 0), dev(y + 1, 0)) for y in range(chips)] + [(dev(y, 1), dev(y - 1, 1)) for y in range(chips)]
    back = [(b, a) for a, b in out]
    cross = [(dev(y, 0), dev(y - 1, 1)) for y in range(chips)] + [(dev(y, 1), dev(y + 1, 0)) for y in range(chips)]
    swap = [(d, d ^ 1) for d in range(2 * chips)]
    return out, back, cross, swap


def shift(array, by):
    peers = lax.axis_size("blk")
    return lax.ppermute(array, "blk", [(i, (i + by) % peers) for i in range(peers)])


def local(image_feats, head_weight, text_embeds, positives, logit_scale, logit_bias, loss_scale):
    out, back, cross, swap = ring_maps(lax.axis_size("rep") // 2)
    f32, bf16 = jnp.float32, jnp.bfloat16
    me = lax.axis_index("rep")
    chip, core = me // 2, me % 2

    def rep(array, pairs):
        return lax.ppermute(array, "rep", pairs)

    place = positives[0]
    digits = jnp.stack([place // 128, place % 128], axis=1).astype(bf16)
    own = jnp.concatenate([image_feats, digits, jnp.zeros((ROWS, WIDE - D - 2), bf16)], axis=1)
    first = [rep(own, out)]
    second = [rep(own, cross)]
    text_one = shift(text_embeds, 1)
    text_two = shift(text_embeds, 2)
    for k in range(3):
        first.append(rep(first[-1], out))
        if k < 2:
            second.append(rep(second[-1], out))

    text_own = rep(text_embeds, swap)
    far = rep(jnp.concatenate([text_one, text_two], axis=0), swap)
    raw = jnp.concatenate([text_embeds, text_own, text_one, far[:ROWS], text_two, far[ROWS:]], axis=0)
    texts = unit_of(raw.astype(f32))[0].astype(bf16)

    temper = logit_scale[0]
    scal = jnp.stack(
        [
            temper,
            logit_bias[0],
            loss_scale[0] * temper,
            (me * ROWS).astype(f32),
            ((me + 1 - 2 * core) * ROWS).astype(f32),
        ]
    )
    groups = [[own, first[0], second[0]], [first[1], second[1]], [first[2], second[2]], [first[3]]]
    terms = [tile_terms(scal, head_weight, texts, group) for group in groups]
    tiles = [tile for group in groups for tile in group]
    parts = [t[0][n : n + ROWS] for t in terms for n in range(0, t[0].shape[0], ROWS)]

    way = 1 - 2 * core
    here = [me]
    there = [me + way]
    for k in (1, 2, 3, 4):
        below, above = (chip - way * k) % 8, (chip + way * k) % 8
        here += [2 * below + core] + ([2 * below + 1 - core] if k < 4 else [])
        there += [2 * above + 1 - core] + ([2 * above + core] if k < 4 else [])
    index = jnp.stack(here + there).astype(jnp.int32)
    head_mine, head_other = head_terms(index, tiles, [t[1] for t in terms])
    head_sum = head_mine + rep(head_other, swap).astype(f32)

    text_mine, text_other = text_terms([t[3] for t in terms], [t[2] for t in terms])
    text_sum = text_mine + rep(text_other, swap).astype(f32)
    text_total = (
        text_sum[0]
        + shift(text_sum[1].astype(bf16), -1).astype(f32)
        + shift(text_sum[2].astype(bf16), -2).astype(f32)
    )

    def message(n):
        return jnp.concatenate([parts[n].astype(f32), head_sum[n]], axis=0)

    a_sum = rep(message(7).astype(bf16), back)
    b_sum = rep(message(6).astype(bf16), back)
    a_sum = rep((a_sum.astype(f32) + message(5)).astype(bf16), back)
    b_sum = rep((b_sum.astype(f32) + message(4)).astype(bf16), back)
    a_sum = rep((a_sum.astype(f32) + message(3)).astype(bf16), back)
    b_sum = rep((b_sum.astype(f32) + message(2)).astype(bf16), cross)
    a_sum = rep((a_sum.astype(f32) + message(1)).astype(bf16), back)
    total = message(0) + a_sum.astype(f32) + b_sum.astype(f32)

    hidden = jnp.dot(image_feats, head_weight, preferred_element_type=f32)
    unit, scale = unit_of(hidden)
    hidden_grad = unit_pull(unit, scale, total[:ROWS]).astype(bf16)
    image_grads = lax.dot_general(hidden_grad, head_weight, ROWS_BY_ROWS, preferred_element_type=f32).astype(bf16)
    head_grad = total[ROWS:][None]
    text_unit, text_scale = unit_of(text_embeds.astype(f32))
    text_grads = unit_pull(text_unit, text_scale, text_total).astype(bf16)
    return (image_grads, text_grads, head_grad)


def solution(mesh):
    placed = (P(("blk", "rep"), None), P(), P(("blk", "rep"), None), P("blk", "rep"), P(), P(), P())
    return jax.shard_map(
        local,
        mesh=mesh,
        in_specs=placed,
        out_specs=(P(("blk", "rep"), None), P(("blk", "rep"), None), P("blk", "rep", None)),
        check_vma=False,
    )
```

```python
import functools
import math

import jax
import jax.numpy as jnp
from jax import lax
from jax.experimental import pallas as pl
from jax.experimental.pallas import tpu as pltpu
from jax.sharding import PartitionSpec as P

STEPS = 3
EPSILON = 1e-06
D = 1152
ROWS = 128
WIDE = 1280
SLICE = 72
VMEM_LIMIT = 20 * 1024 * 1024
ROOT = 1.0 / math.sqrt(D)

ROWS_BY_ROWS = (((1,), (1,)), ((), ()))
DEPTH_FIRST = (((0,), (0,)), ((), ()))


def unit_of(values):
    scale = lax.rsqrt(jnp.mean(values * values, axis=-1, keepdims=True) + EPSILON) * ROOT
    return values * scale, scale


def unit_pull(unit, scale, grad):
    return scale * (grad - unit * jnp.sum(unit * grad, axis=-1, keepdims=True))


def whole(count):
    return [pl.BlockSpec(memory_space=pltpu.VMEM)] * count


def call(kernel, out_shape, operands, scalars, flops, scratch=()):
    moved = sum(math.prod(a.shape) * a.dtype.itemsize for a in list(operands) + list(out_shape))
    return pl.pallas_call(
        kernel,
        out_shape=out_shape,
        in_specs=[pl.BlockSpec(memory_space=pltpu.SMEM)] * len(scalars) + whole(len(operands)),
        out_specs=whole(len(out_shape)),
        scratch_shapes=list(scratch),
        compiler_params=pltpu.CompilerParams(vmem_limit_bytes=VMEM_LIMIT),
        cost_estimate=pl.CostEstimate(flops=0, bytes_accessed=1, transcendentals=0),
    )(*scalars, *operands)


def prepare_kernel(feats, place, wide):
    row = lax.broadcasted_iota(jnp.int32, (ROWS, ROWS), 0)
    lane = lax.broadcasted_iota(jnp.int32, (ROWS, ROWS), 1)
    here = jnp.where(row == lane, place[...].astype(jnp.float32), 0.0)
    column = jnp.sum(here, axis=1, keepdims=True).astype(jnp.int32)
    digits = jnp.where(lane == 0, column // 128, jnp.where(lane == 1, column % 128, 0))
    wide[:, :D] = feats[...]
    wide[:, D:] = digits.astype(jnp.float32).astype(jnp.bfloat16)


def prepare(feats, place):
    return call(prepare_kernel, [bf16_shape(ROWS, WIDE)], [feats, place], [], 0)[0]


def bf16_shape(*shape):
    return jax.ShapeDtypeStruct(shape, jnp.bfloat16)


def f32_shape(*shape):
    return jax.ShapeDtypeStruct(shape, jnp.float32)


def text_unit_kernel(*refs):
    mine, other, out = refs[:STEPS], refs[STEPS], refs[STEPS + 1]
    for n in range(2 * STEPS):
        raw = mine[n // 2][...] if n % 2 == 0 else other[n // 2]
        out[n * ROWS : (n + 1) * ROWS, :] = unit_of(raw.astype(jnp.float32))[0].astype(jnp.bfloat16)


def side_kernel(*refs):
    for n, ref in enumerate(refs[:-1]):
        refs[-1][n] = ref[...]


def side_by_side(pieces):
    return call(side_kernel, [bf16_shape(len(pieces), ROWS, D)], pieces, [], 0)[0]


def text_units(mine, other):
    return call(text_unit_kernel, [bf16_shape(2 * STEPS * ROWS, D)], [*mine, other], [], 0)[0]


def rows_of(tiles):
    return sum(t.shape[0] for t in tiles)


def gather_feats(tiles):
    return jnp.concatenate([t[:, :D] for t in tiles], axis=0) if len(tiles) > 1 else tiles[0][:, :D]


def unit_kernel(count, weight, *refs):
    tiles, (low_ref, scale_ref, turned_ref, *first) = refs[:count], refs[count:]
    feats = gather_feats(tiles)
    unit, scale = unit_of(jnp.dot(feats, weight[...], preferred_element_type=jnp.float32))
    low_ref[...] = unit.astype(jnp.bfloat16)
    scale_ref[...] = jnp.broadcast_to(scale, scale_ref.shape)
    turned_ref[...] = feats.T
    for copy in first:
        copy[...] = tiles[0][:ROWS, :]


def image_units(weight, tiles, first=0):
    rows = rows_of(tiles)
    return call(
        functools.partial(unit_kernel, len(tiles)),
        [bf16_shape(rows, D), f32_shape(rows, 128), bf16_shape(D, rows)] + [bf16_shape(ROWS, WIDE)] * first,
        [weight, *tiles],
        [],
        2 * rows * D * D,
    )


def band(scalars, low, scale, place, texts, part_ref, grad_ref, turned_ref):
    temper, offset_bias, loss_scale = (s[0] for s in scalars)
    weighting = loss_scale * temper
    me = lax.axis_index("rep")
    mine = (me * ROWS).astype(jnp.float32)
    other = ((me + 1 - 2 * lax.rem(me, 2)) * ROWS).astype(jnp.float32)
    logits = (
        temper * lax.dot_general(low, texts[...], ROWS_BY_ROWS, preferred_element_type=jnp.float32)
        + offset_bias
    )
    lane = lax.broadcasted_iota(jnp.int32, (1, 2 * STEPS * ROWS), 1)
    spot = jnp.where(lane < 128, mine, other - 128.0) + lane.astype(jnp.float32)
    spot = jnp.where(lane < 256, spot, -1.0)
    match = place == spot
    sigmoid = 1.0 / (1.0 + jnp.exp(jnp.where(match, logits, -logits)))
    coeffs = (jnp.where(match, -weighting, weighting) * sigmoid).astype(jnp.bfloat16)
    turned_ref[...] = coeffs.T
    part = jnp.dot(coeffs, texts[...], preferred_element_type=jnp.float32)
    part_ref[...] = part.astype(jnp.bfloat16)
    unit = low.astype(jnp.float32)
    grad_ref[...] = unit_pull(unit, scale, part).astype(jnp.bfloat16)


def places(tiles):
    digits = [t[:, D:].astype(jnp.float32) for t in tiles]
    return jnp.concatenate([d[:, 0:1] * 128.0 + d[:, 1:2] for d in digits], axis=0)


def band_kernel(count, temper, offset_bias, loss_scale, low, scale, texts, *refs):
    band((temper, offset_bias, loss_scale), low[...], scale[:, 0:1], places(refs[:count]), texts, *refs[count:])


def band_shapes(rows):
    return [bf16_shape(rows, D), bf16_shape(rows, D), bf16_shape(2 * STEPS * ROWS, rows)]


def band_terms(scalars, low, scale, texts, tiles):
    rows = rows_of(tiles)
    return call(
        functools.partial(band_kernel, len(tiles)),
        band_shapes(rows),
        [low, scale, texts, *tiles],
        scalars,
        8 * rows * D * STEPS * ROWS,
    )


CUTS = ((0, 512), (512, 640))


def lay_out(lefts, rights, wide, deep):
    at = 0
    for left, right in zip(lefts, rights):
        rows = right.shape[0]
        wide[:, at : at + rows] = left[...]
        deep[at : at + rows, :] = right[...]
        at += rows


def slice_numbers():
    me = lax.axis_index("rep")
    core = lax.rem(me, 2)
    chip = (me - core) // 2
    way = 1 - 2 * core
    here, there = [me], [me + way]
    for k in (1, 2, 3, 4):
        below, above = lax.rem(chip - way * k + 8, 8), lax.rem(chip + way * k + 8, 8)
        here += [2 * below + core] + ([2 * below + 1 - core] if k < 4 else [])
        there += [2 * above + 1 - core] + ([2 * above + core] if k < 4 else [])
    return here, there


def head_kernel(count, *refs):
    feats, grads = refs[:count], refs[count : 2 * count]
    mine_ref, other_ref, wide, deep, total = refs[2 * count :]
    lay_out(feats, grads, wide, deep)
    for start, width in CUTS:
        total[:, start : start + width] = jnp.dot(
            wide[...], deep[:, start : start + width], preferred_element_type=jnp.float32
        )
    here, there = slice_numbers()
    for n in range(8):
        mine_ref[n] = total[pl.ds(pl.multiple_of(here[n] * SLICE, 8), SLICE), :].astype(jnp.bfloat16)
        other_ref[n] = total[pl.ds(pl.multiple_of(there[n] * SLICE, 8), SLICE), :].astype(jnp.bfloat16)


def head_terms(feats, grads):
    return call(
        functools.partial(head_kernel, len(feats)),
        [bf16_shape(8, SLICE, D), bf16_shape(8, SLICE, D)],
        [*feats, *grads],
        [],
        2 * 8 * ROWS * D * D,
        [
            pltpu.VMEM((D, 8 * ROWS), jnp.bfloat16),
            pltpu.VMEM((8 * ROWS, D), jnp.bfloat16),
            pltpu.VMEM((D, D), jnp.float32),
        ],
    )


def text_kernel(count, *refs):
    coeffs, units = refs[:count], refs[count : 2 * count]
    mine_ref, other_ref, wide, deep = refs[2 * count :]
    lay_out(coeffs, units, wide, deep)
    for start, width in CUTS:
        columns = slice(start, start + width)
        total = jnp.dot(wide[...], deep[:, columns], preferred_element_type=jnp.float32)
        for k in range(STEPS):
            mine_ref[k, :, columns] = total[2 * k * ROWS : (2 * k + 1) * ROWS]
            other_ref[k, :, columns] = total[(2 * k + 1) * ROWS : (2 * k + 2) * ROWS].astype(jnp.bfloat16)


def text_terms(coeffs, units):
    return call(
        functools.partial(text_kernel, len(coeffs)),
        [f32_shape(STEPS, ROWS, D), bf16_shape(STEPS, ROWS, D)],
        [*coeffs, *units],
        [],
        2 * 8 * ROWS * 2 * STEPS * ROWS * D,
        [pltpu.VMEM((2 * STEPS * ROWS, 8 * ROWS), jnp.bfloat16), pltpu.VMEM((8 * ROWS, D), jnp.bfloat16)],
    )


def text_sum_kernel(mine, other, own, one, two):
    own[...] = mine[0] + other[0].astype(jnp.float32)
    one[...] = (mine[1] + other[1].astype(jnp.float32)).astype(jnp.bfloat16)
    two[...] = (mine[2] + other[2].astype(jnp.float32)).astype(jnp.bfloat16)


def text_sums(mine, other):
    return call(
        text_sum_kernel, [f32_shape(ROWS, D), bf16_shape(ROWS, D), bf16_shape(ROWS, D)], [mine, other], [], 0
    )


def after(values, *others):
    return lax.optimization_barrier((values, others))[0]


def text_grad_kernel(raw, own, one, two, out):
    unit, scale = unit_of(raw[...].astype(jnp.float32))
    total = own[...] + one[...].astype(jnp.float32) + two[...].astype(jnp.float32)
    out[...] = unit_pull(unit, scale, total).astype(jnp.bfloat16)


def final_kernel(weight, low, scale, part, head, a_sum, b_sum, image_out, head_out):
    total = a_sum[...].astype(jnp.float32) + b_sum[...].astype(jnp.float32)
    grad = part[:ROWS, :].astype(jnp.float32) + total[:ROWS]
    unit = low[:ROWS, :].astype(jnp.float32)
    hidden_grad = unit_pull(unit, scale[:ROWS, 0:1], grad).astype(jnp.bfloat16)
    image_out[...] = lax.dot_general(
        hidden_grad, weight[...], ROWS_BY_ROWS, preferred_element_type=jnp.float32
    ).astype(jnp.bfloat16)
    head_out[0] = head[...] + total[ROWS:]


def ring_maps(chips):
    def dev(y, c):
        return 2 * (y % chips) + c

    out = [(dev(y, 0), dev(y + 1, 0)) for y in range(chips)] + [(dev(y, 1), dev(y - 1, 1)) for y in range(chips)]
    back = [(b, a) for a, b in out]
    out_two = [(dev(y, 0), dev(y + 2, 0)) for y in range(chips)] + [(dev(y, 1), dev(y - 2, 1)) for y in range(chips)]
    back_two = [(dev(y, 0), dev(y - 2, 0)) for y in range(chips)] + [(dev(y, 1), dev(y + 2, 1)) for y in range(chips)]
    cross = [(dev(y, 0), dev(y - 1, 1)) for y in range(chips)] + [(dev(y, 1), dev(y + 1, 0)) for y in range(chips)]
    swap = [(d, d ^ 1) for d in range(2 * chips)]
    return out, out_two, back, back_two, cross, swap


def shift(array, by):
    peers = lax.axis_size("blk")
    return lax.ppermute(array, "blk", [(i, (i + by) % peers) for i in range(peers)])


def local(image_feats, head_weight, text_embeds, positives, logit_scale, logit_bias, loss_scale):
    out, out_two, back, back_two, cross, swap = ring_maps(lax.axis_size("rep") // 2)
    f32, bf16 = jnp.float32, jnp.bfloat16

    def rep(array, pairs):
        return lax.ppermute(array, "rep", pairs)

    own = prepare(image_feats, positives)
    a_one, b_one = rep(own, out), rep(own, cross)
    text_one = shift(jnp.pad(text_embeds, ((0, 0), (0, 256))), 1)[:, :D]
    a_one, b_one, text_one = after((a_one, b_one, text_one))
    pair_one = jnp.concatenate([a_one, b_one], axis=0)
    pair_two = rep(pair_one, out)
    text_two = shift(text_one, 1)
    units = [image_units(head_weight, [own, pair_one])]
    pair_two, text_two = after((pair_two, text_two), units[0])
    text_mine = side_by_side([text_embeds, text_one, text_two])
    pair_three = rep(pair_two, out)
    units.append(image_units(head_weight, [pair_two], 1))
    a_four = rep(units[1][3], out_two)
    texts = text_units([text_embeds, text_one, text_two], rep(text_mine, swap))

    scalars = [logit_scale, logit_bias, loss_scale]
    groups = [[own, pair_one], [pair_two]]
    terms = [band_terms(scalars, u[0], u[1], texts, group) for u, group in zip(units, groups)]
    groups.append(after([pair_three, a_four], terms))
    units.append(image_units(head_weight, groups[2]))
    terms.append(band_terms(scalars, units[2][0], units[2][1], texts, groups[2]))
    part_groups = [t[0] for t in terms]
    parts = [p[n : n + ROWS] for p in part_groups for n in range(0, p.shape[0], ROWS)]

    head_mine, head_other = head_terms(
        [u[2] for u in units], [t[1] for t in terms]
    )
    head_sum = head_mine.astype(f32) + rep(head_other, swap).astype(f32)
    text_mine, text_other = text_terms(
        [t[2] for t in terms], [u[0] for u in units]
    )

    def message(n, *came):
        total = jnp.concatenate([parts[n].astype(f32), head_sum[n]], axis=0)
        for other in came:
            total = total + other.astype(f32)
        return total.astype(bf16)

    a_sum, b_sum = rep(message(7), back), rep(message(6), back)
    text_came = after(rep(text_other, swap), a_sum)
    text_own, text_one_sum, text_two_sum = text_sums(text_mine, text_came)
    one_came, two_came = shift(text_one_sum, -1), shift(text_two_sum, -2)
    a_sum, b_sum = rep(message(5, a_sum), back), rep(message(4, b_sum), back)
    a_sum, b_sum = rep(message(3, a_sum), back), rep(message(2, b_sum), cross)
    a_sum = after(a_sum, one_came, two_came)
    a_sum = rep(message(1, a_sum), back)
    image_grads, head_grad = call(
        final_kernel,
        [bf16_shape(ROWS, D), f32_shape(1, SLICE, D)],
        [head_weight, units[0][0], units[0][1], part_groups[0], head_sum[0], a_sum, b_sum],
        [],
        2 * ROWS * D * D,
    )
    (text_grads,) = call(
        text_grad_kernel,
        [bf16_shape(ROWS, D)],
        [text_embeds, text_own, one_came, two_came],
        [],
        0,
    )
    return (image_grads, text_grads, head_grad)


def solution(mesh):
    placed = (P(("blk", "rep"), None), P(), P(("blk", "rep"), None), P("blk", "rep"), P(), P(), P())
    return jax.shard_map(
        local,
        mesh=mesh,
        in_specs=placed,
        out_specs=(P(("blk", "rep"), None), P(("blk", "rep"), None), P("blk", "rep", None)),
        check_vma=False,
    )
```

```python
import functools
import math

import jax
import jax.numpy as jnp
from jax import lax
from jax.experimental import pallas as pl
from jax.experimental.pallas import tpu as pltpu
from jax.sharding import PartitionSpec as P

STEPS = 3
EPSILON = 1e-06
D = 1152
ROWS = 128
WIDE = 1280
SLICE = 72
VMEM_LIMIT = 20 * 1024 * 1024
ROOT = 1.0 / math.sqrt(D)

ROWS_BY_ROWS = (((1,), (1,)), ((), ()))
DEPTH_FIRST = (((0,), (0,)), ((), ()))


def unit_of(values):
    scale = lax.rsqrt(jnp.mean(values * values, axis=-1, keepdims=True) + EPSILON) * ROOT
    return values * scale, scale


def unit_pull(unit, scale, grad):
    return scale * (grad - unit * jnp.sum(unit * grad, axis=-1, keepdims=True))


def whole(count):
    return [pl.BlockSpec(memory_space=pltpu.VMEM)] * count


def call(kernel, out_shape, operands, scalars, flops, scratch=()):
    moved = sum(math.prod(a.shape) * a.dtype.itemsize for a in list(operands) + list(out_shape))
    return pl.pallas_call(
        kernel,
        out_shape=out_shape,
        in_specs=[pl.BlockSpec(memory_space=pltpu.SMEM)] * len(scalars) + whole(len(operands)),
        out_specs=whole(len(out_shape)),
        scratch_shapes=list(scratch),
        compiler_params=pltpu.CompilerParams(vmem_limit_bytes=VMEM_LIMIT),
        cost_estimate=pl.CostEstimate(flops=0, bytes_accessed=1, transcendentals=0),
    )(*scalars, *operands)


def prepare_kernel(feats, place, wide):
    row = lax.broadcasted_iota(jnp.int32, (ROWS, ROWS), 0)
    lane = lax.broadcasted_iota(jnp.int32, (ROWS, ROWS), 1)
    here = jnp.where(row == lane, place[...].astype(jnp.float32), 0.0)
    column = jnp.sum(here, axis=1, keepdims=True).astype(jnp.int32)
    digits = jnp.where(lane == 0, column // 128, jnp.where(lane == 1, column % 128, 0))
    wide[:, :D] = feats[...]
    wide[:, D:] = digits.astype(jnp.float32).astype(jnp.bfloat16)


def prepare(feats, place):
    return call(prepare_kernel, [bf16_shape(ROWS, WIDE)], [feats, place], [], 0)[0]


def bf16_shape(*shape):
    return jax.ShapeDtypeStruct(shape, jnp.bfloat16)


def f32_shape(*shape):
    return jax.ShapeDtypeStruct(shape, jnp.float32)


def text_unit_kernel(*refs):
    mine, near, far, out = refs[:STEPS], refs[STEPS], refs[STEPS + 1], refs[STEPS + 2]
    for n in range(2 * STEPS):
        other = near[n // 2] if n < 4 else far[...]
        raw = mine[n // 2][:, :D] if n % 2 == 0 else other
        out[n * ROWS : (n + 1) * ROWS, :] = unit_of(raw.astype(jnp.float32))[0].astype(jnp.bfloat16)


def side_kernel(*refs):
    for n, ref in enumerate(refs[:-1]):
        refs[-1][n] = ref[:, :D]


def side_by_side(pieces):
    return call(side_kernel, [bf16_shape(len(pieces), ROWS, D)], pieces, [], 0)[0]


def text_units(mine, other):
    return call(text_unit_kernel, [bf16_shape(2 * STEPS * ROWS, D)], [*mine, *other], [], 0)[0]


def rows_of(tiles):
    return sum(t.shape[0] for t in tiles)


def gather_feats(tiles):
    return jnp.concatenate([t[:, :D] for t in tiles], axis=0) if len(tiles) > 1 else tiles[0][:, :D]


def unit_kernel(count, weight, *refs):
    tiles, (low_ref, scale_ref, turned_ref, *first) = refs[:count], refs[count:]
    feats = gather_feats(tiles)
    unit, scale = unit_of(jnp.dot(feats, weight[...], preferred_element_type=jnp.float32))
    low_ref[...] = unit.astype(jnp.bfloat16)
    scale_ref[...] = jnp.broadcast_to(scale, scale_ref.shape)
    turned_ref[...] = feats.T
    for copy in first:
        copy[...] = tiles[0][:ROWS, :]


def image_units(weight, tiles, first=0):
    rows = rows_of(tiles)
    return call(
        functools.partial(unit_kernel, len(tiles)),
        [bf16_shape(rows, D), f32_shape(rows, 128), bf16_shape(D, rows)] + [bf16_shape(ROWS, WIDE)] * first,
        [weight, *tiles],
        [],
        2 * rows * D * D,
    )


def scalar_kernel(temper, offset_bias, loss_scale, out):
    row = lax.broadcasted_iota(jnp.int32, out.shape, 0)
    lower = jnp.where(row == 0, temper[0], offset_bias[0])
    out[...] = jnp.where(row < 2, lower, loss_scale[0] * temper[0])


def scalar_rows(temper, offset_bias, loss_scale):
    return call(scalar_kernel, [f32_shape(8, 128)], [], [temper, offset_bias, loss_scale], 0)[0]


def band(scalars, low, scale, place, texts, part_ref, grad_ref, turned_ref):
    temper, offset_bias, weighting = (scalars[n : n + 1, 0:1] for n in range(3))
    me = lax.axis_index("rep")
    mine = (me * ROWS).astype(jnp.float32)
    other = ((me + 1 - 2 * lax.rem(me, 2)) * ROWS).astype(jnp.float32)
    logits = (
        temper * lax.dot_general(low, texts[...], ROWS_BY_ROWS, preferred_element_type=jnp.float32)
        + offset_bias
    )
    lane = lax.broadcasted_iota(jnp.int32, (1, 2 * STEPS * ROWS), 1)
    spot = jnp.where(lane < 128, mine, other - 128.0) + lane.astype(jnp.float32)
    spot = jnp.where(lane < 256, spot, -1.0)
    match = place == spot
    sigmoid = 1.0 / (1.0 + jnp.exp(jnp.where(match, logits, -logits)))
    coeffs = (jnp.where(match, -weighting, weighting) * sigmoid).astype(jnp.bfloat16)
    turned_ref[...] = coeffs.T
    part = jnp.dot(coeffs, texts[...], preferred_element_type=jnp.float32)
    part_ref[...] = part.astype(jnp.bfloat16)
    unit = low.astype(jnp.float32)
    grad_ref[...] = unit_pull(unit, scale, part).astype(jnp.bfloat16)


def places(tiles):
    digits = [t[:, D:].astype(jnp.float32) for t in tiles]
    return jnp.concatenate([d[:, 0:1] * 128.0 + d[:, 1:2] for d in digits], axis=0)


def band_kernel(count, scalars, low, scale, texts, *refs):
    band(scalars, low[...], scale[:, 0:1], places(refs[:count]), texts, *refs[count:])


def band_shapes(rows):
    return [bf16_shape(rows, D), bf16_shape(rows, D), bf16_shape(2 * STEPS * ROWS, rows)]


def band_terms(scalars, low, scale, texts, tiles):
    rows = rows_of(tiles)
    return call(
        functools.partial(band_kernel, len(tiles)),
        band_shapes(rows),
        [scalars, low, scale, texts, *tiles],
        [],
        8 * rows * D * STEPS * ROWS,
    )


CUTS = ((0, 512), (512, 640))


def lay_out(lefts, rights, wide, deep):
    at = 0
    for left, right in zip(lefts, rights):
        rows = right.shape[0]
        wide[:, at : at + rows] = left[...]
        deep[at : at + rows, :] = right[...]
        at += rows


def slice_numbers():
    me = lax.axis_index("rep")
    core = lax.rem(me, 2)
    chip = (me - core) // 2
    way = 1 - 2 * core
    here, there = [me], [me + way]
    for k in (1, 2, 3, 4):
        below, above = lax.rem(chip - way * k + 8, 8), lax.rem(chip + way * k + 8, 8)
        here += [2 * below + core] + ([2 * below + 1 - core] if k < 4 else [])
        there += [2 * above + 1 - core] + ([2 * above + core] if k < 4 else [])
    return here, there


def head_kernel(count, *refs):
    feats, grads = refs[:count], refs[count : 2 * count]
    mine_ref, other_ref, wide, deep, total = refs[2 * count :]
    lay_out(feats, grads, wide, deep)
    for start, width in CUTS:
        total[:, start : start + width] = jnp.dot(
            wide[...], deep[:, start : start + width], preferred_element_type=jnp.float32
        )
    here, there = slice_numbers()
    for n in range(8):
        mine_ref[n] = total[pl.ds(pl.multiple_of(here[n] * SLICE, 8), SLICE), :].astype(jnp.bfloat16)
        other_ref[n] = total[pl.ds(pl.multiple_of(there[n] * SLICE, 8), SLICE), :].astype(jnp.bfloat16)


def head_terms(feats, grads):
    return call(
        functools.partial(head_kernel, len(feats)),
        [bf16_shape(8, SLICE, D), bf16_shape(8, SLICE, D)],
        [*feats, *grads],
        [],
        2 * 8 * ROWS * D * D,
        [
            pltpu.VMEM((D, 8 * ROWS), jnp.bfloat16),
            pltpu.VMEM((8 * ROWS, D), jnp.bfloat16),
            pltpu.VMEM((D, D), jnp.float32),
        ],
    )


def text_kernel(count, *refs):
    coeffs, units = refs[:count], refs[count : 2 * count]
    mine_ref, other_ref, wide, deep = refs[2 * count :]
    lay_out(coeffs, units, wide, deep)
    for start, width in CUTS:
        columns = slice(start, start + width)
        total = jnp.dot(wide[...], deep[:, columns], preferred_element_type=jnp.float32)
        for k in range(STEPS):
            mine_ref[k, :, columns] = total[2 * k * ROWS : (2 * k + 1) * ROWS]
            other_ref[k, :, columns] = total[(2 * k + 1) * ROWS : (2 * k + 2) * ROWS].astype(jnp.bfloat16)


def text_terms(coeffs, units):
    return call(
        functools.partial(text_kernel, len(coeffs)),
        [f32_shape(STEPS, ROWS, D), bf16_shape(STEPS, ROWS, D)],
        [*coeffs, *units],
        [],
        2 * 8 * ROWS * 2 * STEPS * ROWS * D,
        [pltpu.VMEM((2 * STEPS * ROWS, 8 * ROWS), jnp.bfloat16), pltpu.VMEM((8 * ROWS, D), jnp.bfloat16)],
    )


def text_sum_kernel(mine, other, own, one, two):
    own[...] = mine[0] + other[0].astype(jnp.float32)
    one[...] = (mine[1] + other[1].astype(jnp.float32)).astype(jnp.bfloat16)
    two[...] = (mine[2] + other[2].astype(jnp.float32)).astype(jnp.bfloat16)


def text_sums(mine, other):
    return call(
        text_sum_kernel, [f32_shape(ROWS, D), bf16_shape(ROWS, D), bf16_shape(ROWS, D)], [mine, other], [], 0
    )


def after(values, *others):
    return lax.optimization_barrier((values, others))[0]


def text_grad_kernel(raw, own, one, two, out):
    unit, scale = unit_of(raw[...].astype(jnp.float32))
    total = own[...] + one[...].astype(jnp.float32) + two[...].astype(jnp.float32)
    out[...] = unit_pull(unit, scale, total).astype(jnp.bfloat16)


def final_kernel(weight, low, scale, part, head, a_sum, b_sum, image_out, head_out):
    total = a_sum[...].astype(jnp.float32) + b_sum[...].astype(jnp.float32)
    grad = part[:ROWS, :].astype(jnp.float32) + total[:ROWS]
    unit = low[:ROWS, :].astype(jnp.float32)
    hidden_grad = unit_pull(unit, scale[:ROWS, 0:1], grad).astype(jnp.bfloat16)
    image_out[...] = lax.dot_general(
        hidden_grad, weight[...], ROWS_BY_ROWS, preferred_element_type=jnp.float32
    ).astype(jnp.bfloat16)
    head_out[0] = head[...] + total[ROWS:]


def ring_maps(chips):
    def dev(y, c):
        return 2 * (y % chips) + c

    out = [(dev(y, 0), dev(y + 1, 0)) for y in range(chips)] + [(dev(y, 1), dev(y - 1, 1)) for y in range(chips)]
    back = [(b, a) for a, b in out]
    out_two = [(dev(y, 0), dev(y + 2, 0)) for y in range(chips)] + [(dev(y, 1), dev(y - 2, 1)) for y in range(chips)]
    back_two = [(dev(y, 0), dev(y - 2, 0)) for y in range(chips)] + [(dev(y, 1), dev(y + 2, 1)) for y in range(chips)]
    cross = [(dev(y, 0), dev(y - 1, 1)) for y in range(chips)] + [(dev(y, 1), dev(y + 1, 0)) for y in range(chips)]
    swap = [(d, d ^ 1) for d in range(2 * chips)]
    return out, out_two, back, back_two, cross, swap


def shift(array, by):
    peers = lax.axis_size("blk")
    return lax.ppermute(array, "blk", [(i, (i + by) % peers) for i in range(peers)])


def local(image_feats, head_weight, text_embeds, positives, logit_scale, logit_bias, loss_scale):
    out, out_two, back, back_two, cross, swap = ring_maps(lax.axis_size("rep") // 2)
    f32, bf16 = jnp.float32, jnp.bfloat16

    def rep(array, pairs):
        return lax.ppermute(array, "rep", pairs)

    own = prepare(image_feats, positives)
    a_one, b_one = rep(own, out), rep(own, cross)
    text_one = shift(jnp.pad(text_embeds, ((0, 0), (0, 256))), 1)
    a_one, b_one, text_one = after((a_one, b_one, text_one))
    pair_one = jnp.concatenate([a_one, b_one], axis=0)
    pair_two = rep(pair_one, out)
    text_two = shift(text_one, 1)
    units = [image_units(head_weight, [own, pair_one])]
    scalars = scalar_rows(logit_scale, logit_bias, loss_scale)
    pair_two = after(pair_two, units[0], scalars)
    pair_three = rep(pair_two, out)
    units.append(image_units(head_weight, [pair_two], 1))
    a_four = rep(units[1][3], out_two)
    near = rep(side_by_side([text_embeds, text_one]), swap)
    text_two = after(text_two, units, near)
    far = rep(text_two[:, :D], swap)
    pair_three, far = after((pair_three, far))
    texts = text_units([text_embeds, text_one, text_two], [near, far])

    groups = [[own, pair_one], [pair_two], [pair_three], [a_four]]
    terms = [band_terms(scalars, u[0], u[1], texts, group) for u, group in zip(units, groups)]
    groups[2] = [after(pair_three, terms)]
    units.append(image_units(head_weight, groups[2]))
    terms.append(band_terms(scalars, units[2][0], units[2][1], texts, groups[2]))
    groups[3] = [after(a_four, terms)]
    units.append(image_units(head_weight, groups[3]))
    terms.append(band_terms(scalars, units[3][0], units[3][1], texts, groups[3]))
    part_groups = [t[0] for t in terms]
    parts = [p[n : n + ROWS] for p in part_groups for n in range(0, p.shape[0], ROWS)]

    head_mine, head_other = head_terms(
        [u[2] for u in units], [t[1] for t in terms]
    )
    head_sum = head_mine.astype(f32) + rep(head_other, swap).astype(f32)
    text_mine, text_other = text_terms(
        [t[2] for t in terms], [u[0] for u in units]
    )

    def message(n, *came):
        total = jnp.concatenate([parts[n].astype(f32), head_sum[n]], axis=0)
        for other in came:
            total = total + other.astype(f32)
        return total.astype(bf16)

    a_sum, b_sum = rep(message(7), back), rep(message(6), back)
    text_came = after(rep(text_other, swap), a_sum)
    text_own, text_one_sum, text_two_sum = text_sums(text_mine, text_came)
    one_came, two_came = shift(text_one_sum, -1), shift(text_two_sum, -2)
    a_sum, b_sum = rep(message(5, a_sum), back), rep(message(4, b_sum), back)
    a_sum, b_sum = rep(message(3, a_sum), back), rep(message(2, b_sum), cross)
    a_sum = after(a_sum, one_came, two_came)
    a_sum = rep(message(1, a_sum), back)
    image_grads, head_grad = call(
        final_kernel,
        [bf16_shape(ROWS, D), f32_shape(1, SLICE, D)],
        [head_weight, units[0][0], units[0][1], part_groups[0], head_sum[0], a_sum, b_sum],
        [],
        2 * ROWS * D * D,
    )
    (text_grads,) = call(
        text_grad_kernel,
        [bf16_shape(ROWS, D)],
        [text_embeds, text_own, one_came, two_came],
        [],
        0,
    )
    return (image_grads, text_grads, head_grad)


def solution(mesh):
    placed = (P(("blk", "rep"), None), P(), P(("blk", "rep"), None), P("blk", "rep"), P(), P(), P())
    return jax.shard_map(
        local,
        mesh=mesh,
        in_specs=placed,
        out_specs=(P(("blk", "rep"), None), P(("blk", "rep"), None), P("blk", "rep", None)),
        check_vma=False,
    )
```

```python
import functools
import math

import jax
import jax.numpy as jnp
from jax import lax
from jax.experimental import pallas as pl
from jax.experimental.pallas import tpu as pltpu
from jax.sharding import PartitionSpec as P

STEPS = 3
EPSILON = 1e-06
D = 1152
ROWS = 128
WIDE = 1280
SLICE = 72
VMEM_LIMIT = 20 * 1024 * 1024
ROOT = 1.0 / math.sqrt(D)

ROWS_BY_ROWS = (((1,), (1,)), ((), ()))
DEPTH_FIRST = (((0,), (0,)), ((), ()))


def unit_of(values):
    scale = lax.rsqrt(jnp.mean(values * values, axis=-1, keepdims=True) + EPSILON) * ROOT
    return values * scale, scale


def unit_pull(unit, scale, grad):
    return scale * (grad - unit * jnp.sum(unit * grad, axis=-1, keepdims=True))


def whole(count):
    return [pl.BlockSpec(memory_space=pltpu.VMEM)] * count


def call(kernel, out_shape, operands, scalars, flops, scratch=()):
    moved = sum(math.prod(a.shape) * a.dtype.itemsize for a in list(operands) + list(out_shape))
    return pl.pallas_call(
        kernel,
        out_shape=out_shape,
        in_specs=[pl.BlockSpec(memory_space=pltpu.SMEM)] * len(scalars) + whole(len(operands)),
        out_specs=whole(len(out_shape)),
        scratch_shapes=list(scratch),
        compiler_params=pltpu.CompilerParams(vmem_limit_bytes=VMEM_LIMIT),
        cost_estimate=pl.CostEstimate(flops=0, bytes_accessed=1, transcendentals=0),
    )(*scalars, *operands)


def prepare_kernel(feats, place, wide):
    row = lax.broadcasted_iota(jnp.int32, (ROWS, ROWS), 0)
    lane = lax.broadcasted_iota(jnp.int32, (ROWS, ROWS), 1)
    here = jnp.where(row == lane, place[...].astype(jnp.float32), 0.0)
    column = jnp.sum(here, axis=1, keepdims=True).astype(jnp.int32)
    digits = jnp.where(lane == 0, column // 128, jnp.where(lane == 1, column % 128, 0))
    wide[:, :D] = feats[...]
    wide[:, D:] = digits.astype(jnp.float32).astype(jnp.bfloat16)


def prepare(feats, place):
    return call(prepare_kernel, [bf16_shape(ROWS, WIDE)], [feats, place], [], 0)[0]


def bf16_shape(*shape):
    return jax.ShapeDtypeStruct(shape, jnp.bfloat16)


def f32_shape(*shape):
    return jax.ShapeDtypeStruct(shape, jnp.float32)


def text_unit_kernel(*refs):
    mine, near, far, out = refs[:STEPS], refs[STEPS], refs[STEPS + 1], refs[STEPS + 2]
    for n in range(2 * STEPS):
        other = near[n // 2] if n < 4 else far[...]
        raw = mine[n // 2][:, :D] if n % 2 == 0 else other
        out[n * ROWS : (n + 1) * ROWS, :] = unit_of(raw.astype(jnp.float32))[0].astype(jnp.bfloat16)


def side_kernel(*refs):
    for n, ref in enumerate(refs[:-1]):
        refs[-1][n] = ref[:, :D]


def side_by_side(pieces):
    return call(side_kernel, [bf16_shape(len(pieces), ROWS, D)], pieces, [], 0)[0]


def text_units(mine, other):
    return call(text_unit_kernel, [bf16_shape(2 * STEPS * ROWS, D)], [*mine, *other], [], 0)[0]


def rows_of(tiles):
    return sum(t.shape[0] for t in tiles)


def gather_feats(tiles):
    return jnp.concatenate([t[:, :D] for t in tiles], axis=0) if len(tiles) > 1 else tiles[0][:, :D]


def unit_kernel(count, weight, *refs):
    tiles, (low_ref, scale_ref, turned_ref, *first) = refs[:count], refs[count:]
    feats = gather_feats(tiles)
    unit, scale = unit_of(jnp.dot(feats, weight[...], preferred_element_type=jnp.float32))
    low_ref[...] = unit.astype(jnp.bfloat16)
    scale_ref[...] = jnp.broadcast_to(scale, scale_ref.shape)
    turned_ref[...] = feats.T
    for copy in first:
        copy[...] = tiles[0][:ROWS, :]


def image_units(weight, tiles, first=0):
    rows = rows_of(tiles)
    return call(
        functools.partial(unit_kernel, len(tiles)),
        [bf16_shape(rows, D), f32_shape(rows, 128), bf16_shape(D, rows)] + [bf16_shape(ROWS, WIDE)] * first,
        [weight, *tiles],
        [],
        2 * rows * D * D,
    )


def scalar_kernel(temper, offset_bias, loss_scale, out):
    row = lax.broadcasted_iota(jnp.int32, out.shape, 0)
    lower = jnp.where(row == 0, temper[0], offset_bias[0])
    out[...] = jnp.where(row < 2, lower, loss_scale[0] * temper[0])


def scalar_rows(temper, offset_bias, loss_scale):
    return call(scalar_kernel, [f32_shape(8, 128)], [], [temper, offset_bias, loss_scale], 0)[0]


def band(scalars, low, scale, place, texts, part_ref, grad_ref, turned_ref):
    temper, offset_bias, weighting = (scalars[n : n + 1, 0:1] for n in range(3))
    me = lax.axis_index("rep")
    mine = (me * ROWS).astype(jnp.float32)
    other = ((me + 1 - 2 * lax.rem(me, 2)) * ROWS).astype(jnp.float32)
    logits = (
        temper * lax.dot_general(low, texts[...], ROWS_BY_ROWS, preferred_element_type=jnp.float32)
        + offset_bias
    )
    lane = lax.broadcasted_iota(jnp.int32, (1, 2 * STEPS * ROWS), 1)
    spot = jnp.where(lane < 128, mine, other - 128.0) + lane.astype(jnp.float32)
    spot = jnp.where(lane < 256, spot, -1.0)
    match = place == spot
    sigmoid = 1.0 / (1.0 + jnp.exp(jnp.where(match, logits, -logits)))
    coeffs = (jnp.where(match, -weighting, weighting) * sigmoid).astype(jnp.bfloat16)
    turned_ref[...] = coeffs.T
    part = jnp.dot(coeffs, texts[...], preferred_element_type=jnp.float32)
    part_ref[...] = part.astype(jnp.bfloat16)
    unit = low.astype(jnp.float32)
    grad_ref[...] = unit_pull(unit, scale, part).astype(jnp.bfloat16)


def places(tiles):
    digits = [t[:, D:].astype(jnp.float32) for t in tiles]
    return jnp.concatenate([d[:, 0:1] * 128.0 + d[:, 1:2] for d in digits], axis=0)


def band_kernel(count, scalars, low, scale, texts, *refs):
    band(scalars, low[...], scale[:, 0:1], places(refs[:count]), texts, *refs[count:])


def band_shapes(rows):
    return [bf16_shape(rows, D), bf16_shape(rows, D), bf16_shape(2 * STEPS * ROWS, rows)]


def band_terms(scalars, low, scale, texts, tiles):
    rows = rows_of(tiles)
    return call(
        functools.partial(band_kernel, len(tiles)),
        band_shapes(rows),
        [scalars, low, scale, texts, *tiles],
        [],
        8 * rows * D * STEPS * ROWS,
    )


CUTS = ((0, 512), (512, 640))


def lay_out(lefts, rights, wide, deep):
    at = 0
    for left, right in zip(lefts, rights):
        rows = right.shape[0]
        wide[:, at : at + rows] = left[...]
        deep[at : at + rows, :] = right[...]
        at += rows


def slice_numbers():
    me = lax.axis_index("rep")
    core = lax.rem(me, 2)
    chip = (me - core) // 2
    way = 1 - 2 * core
    here, there = [me], [me + way]
    for k in (1, 2, 3, 4):
        below, above = lax.rem(chip - way * k + 8, 8), lax.rem(chip + way * k + 8, 8)
        here += [2 * below + core] + ([2 * below + 1 - core] if k < 4 else [])
        there += [2 * above + 1 - core] + ([2 * above + core] if k < 4 else [])
    return here, there


def head_kernel(count, *refs):
    feats, grads = refs[:count], refs[count : 2 * count]
    mine_ref, other_ref, wide, deep, total = refs[2 * count :]
    lay_out(feats, grads, wide, deep)
    for start, width in CUTS:
        total[:, start : start + width] = jnp.dot(
            wide[...], deep[:, start : start + width], preferred_element_type=jnp.float32
        )
    here, there = slice_numbers()
    for n in range(8):
        mine_ref[n] = total[pl.ds(pl.multiple_of(here[n] * SLICE, 8), SLICE), :].astype(jnp.bfloat16)
        other_ref[n] = total[pl.ds(pl.multiple_of(there[n] * SLICE, 8), SLICE), :].astype(jnp.bfloat16)


def head_terms(feats, grads):
    return call(
        functools.partial(head_kernel, len(feats)),
        [bf16_shape(8, SLICE, D), bf16_shape(8, SLICE, D)],
        [*feats, *grads],
        [],
        2 * 8 * ROWS * D * D,
        [
            pltpu.VMEM((D, 8 * ROWS), jnp.bfloat16),
            pltpu.VMEM((8 * ROWS, D), jnp.bfloat16),
            pltpu.VMEM((D, D), jnp.float32),
        ],
    )


def text_kernel(count, *refs):
    coeffs, units = refs[:count], refs[count : 2 * count]
    mine_ref, other_ref, wide, deep = refs[2 * count :]
    lay_out(coeffs, units, wide, deep)
    for start, width in CUTS:
        columns = slice(start, start + width)
        total = jnp.dot(wide[...], deep[:, columns], preferred_element_type=jnp.float32)
        for k in range(STEPS):
            mine_ref[k, :, columns] = total[2 * k * ROWS : (2 * k + 1) * ROWS]
            other_ref[k, :, columns] = total[(2 * k + 1) * ROWS : (2 * k + 2) * ROWS].astype(jnp.bfloat16)


def text_terms(coeffs, units):
    return call(
        functools.partial(text_kernel, len(coeffs)),
        [f32_shape(STEPS, ROWS, D), bf16_shape(STEPS, ROWS, D)],
        [*coeffs, *units],
        [],
        2 * 8 * ROWS * 2 * STEPS * ROWS * D,
        [pltpu.VMEM((2 * STEPS * ROWS, 8 * ROWS), jnp.bfloat16), pltpu.VMEM((8 * ROWS, D), jnp.bfloat16)],
    )


def text_sum_kernel(mine, other, own, one, two):
    own[...] = mine[0] + other[0].astype(jnp.float32)
    one[...] = (mine[1] + other[1].astype(jnp.float32)).astype(jnp.bfloat16)
    two[...] = (mine[2] + other[2].astype(jnp.float32)).astype(jnp.bfloat16)


def text_sums(mine, other):
    return call(
        text_sum_kernel, [f32_shape(ROWS, D), bf16_shape(ROWS, D), bf16_shape(ROWS, D)], [mine, other], [], 0
    )


def after(values, *others):
    return lax.optimization_barrier((values, others))[0]


def text_grad_kernel(raw, own, one, two, out):
    unit, scale = unit_of(raw[...].astype(jnp.float32))
    total = own[...] + one[...].astype(jnp.float32) + two[...].astype(jnp.float32)
    out[...] = unit_pull(unit, scale, total).astype(jnp.bfloat16)


def final_kernel(weight, low, scale, part, head, a_sum, b_sum, image_out, head_out):
    total = a_sum[...].astype(jnp.float32) + b_sum[...].astype(jnp.float32)
    grad = part[:ROWS, :].astype(jnp.float32) + total[:ROWS]
    unit = low[:ROWS, :].astype(jnp.float32)
    hidden_grad = unit_pull(unit, scale[:ROWS, 0:1], grad).astype(jnp.bfloat16)
    image_out[...] = lax.dot_general(
        hidden_grad, weight[...], ROWS_BY_ROWS, preferred_element_type=jnp.float32
    ).astype(jnp.bfloat16)
    head_out[0] = head[...] + total[ROWS:]


def ring_maps(chips):
    def dev(y, c):
        return 2 * (y % chips) + c

    out = [(dev(y, 0), dev(y + 1, 0)) for y in range(chips)] + [(dev(y, 1), dev(y - 1, 1)) for y in range(chips)]
    back = [(b, a) for a, b in out]
    out_two = [(dev(y, 0), dev(y + 2, 0)) for y in range(chips)] + [(dev(y, 1), dev(y - 2, 1)) for y in range(chips)]
    back_two = [(dev(y, 0), dev(y - 2, 0)) for y in range(chips)] + [(dev(y, 1), dev(y + 2, 1)) for y in range(chips)]
    cross = [(dev(y, 0), dev(y - 1, 1)) for y in range(chips)] + [(dev(y, 1), dev(y + 1, 0)) for y in range(chips)]
    swap = [(d, d ^ 1) for d in range(2 * chips)]
    return out, out_two, back, back_two, cross, swap


def shift(array, by):
    peers = lax.axis_size("blk")
    return lax.ppermute(array, "blk", [(i, (i + by) % peers) for i in range(peers)])


def local(image_feats, head_weight, text_embeds, positives, logit_scale, logit_bias, loss_scale):
    out, out_two, back, back_two, cross, swap = ring_maps(lax.axis_size("rep") // 2)
    f32, bf16 = jnp.float32, jnp.bfloat16

    def rep(array, pairs):
        return lax.ppermute(array, "rep", pairs)

    own = prepare(image_feats, positives)
    a_one, b_one = rep(own, out), rep(own, cross)
    text_one = shift(jnp.pad(text_embeds, ((0, 0), (0, 512))), 1)
    pair_one = jnp.concatenate([a_one, b_one], axis=0)
    pair_two = rep(pair_one, out)
    text_two = shift(text_one[:, :1408], 1)
    pair_held, text_one = after((pair_one, text_one))
    units = [image_units(head_weight, [own, pair_held])]
    scalars = scalar_rows(after(logit_scale, units[0]), logit_bias, loss_scale)
    pair_two = after(pair_two, units[0], scalars)
    pair_three = rep(pair_two, out)
    units.append(image_units(head_weight, [pair_two], 1))
    a_four = rep(units[1][3], out_two)
    near = rep(side_by_side([text_embeds, after(text_one, units[0])]), swap)
    text_two = after(text_two, units, near)
    far = rep(text_two[:, :D], swap)
    pair_three, far = after((pair_three, far))
    texts = text_units([text_embeds, text_one, text_two], [near, far])

    groups = [[own, pair_one], [pair_two], [pair_three], [a_four]]
    terms = [band_terms(scalars, u[0], u[1], texts, group) for u, group in zip(units, groups)]
    groups[2] = [after(pair_three, terms)]
    units.append(image_units(head_weight, groups[2]))
    terms.append(band_terms(scalars, units[2][0], units[2][1], texts, groups[2]))
    groups[3] = [after(a_four, terms)]
    units.append(image_units(head_weight, groups[3]))
    terms.append(band_terms(scalars, units[3][0], units[3][1], texts, groups[3]))
    part_groups = [t[0] for t in terms]
    parts = [p[n : n + ROWS] for p in part_groups for n in range(0, p.shape[0], ROWS)]

    head_mine, head_other = head_terms(
        [u[2] for u in units], [t[1] for t in terms]
    )
    head_sum = head_mine.astype(f32) + rep(head_other, swap).astype(f32)
    text_mine, text_other = text_terms(
        after([t[2] for t in terms], head_other), [u[0] for u in units]
    )

    def message(n, *came):
        total = jnp.concatenate([parts[n].astype(f32), head_sum[n]], axis=0)
        for other in came:
            total = total + other.astype(f32)
        return total.astype(bf16)

    a_sum, b_sum = rep(message(7), back), rep(message(6), back)
    a_next = message(5, a_sum)
    text_came = after(rep(text_other, swap), a_next)
    text_own, text_one_sum, text_two_sum = text_sums(text_mine, text_came)
    one_came, two_came = shift(text_one_sum, -1), shift(text_two_sum, -2)
    a_sum, b_sum = rep(a_next, back), rep(message(4, b_sum), back)
    a_sum, b_sum = rep(message(3, a_sum), back), rep(message(2, b_sum), cross)
    a_sum = after(a_sum, one_came, two_came)
    a_sum = rep(message(1, a_sum), back)
    image_grads, head_grad = call(
        final_kernel,
        [bf16_shape(ROWS, D), f32_shape(1, SLICE, D)],
        [head_weight, units[0][0], units[0][1], part_groups[0], head_sum[0], a_sum, b_sum],
        [],
        2 * ROWS * D * D,
    )
    (text_grads,) = call(
        text_grad_kernel,
        [bf16_shape(ROWS, D)],
        [text_embeds, text_own, one_came, two_came],
        [],
        0,
    )
    return (image_grads, text_grads, head_grad)


def solution(mesh):
    placed = (P(("blk", "rep"), None), P(), P(("blk", "rep"), None), P("blk", "rep"), P(), P(), P())
    return jax.shard_map(
        local,
        mesh=mesh,
        in_specs=placed,
        out_specs=(P(("blk", "rep"), None), P(("blk", "rep"), None), P("blk", "rep", None)),
        check_vma=False,
    )
```

```python
import functools
import math

import jax
import jax.numpy as jnp
from jax import lax
from jax.experimental import pallas as pl
from jax.experimental.pallas import tpu as pltpu
from jax.sharding import PartitionSpec as P

STEPS = 3
EPSILON = 1e-06
D = 1152
ROWS = 128
WIDE = 1280
SLICE = 72
VMEM_LIMIT = 20 * 1024 * 1024
ROOT = 1.0 / math.sqrt(D)

ROWS_BY_ROWS = (((1,), (1,)), ((), ()))
DEPTH_FIRST = (((0,), (0,)), ((), ()))


def unit_of(values):
    scale = lax.rsqrt(jnp.mean(values * values, axis=-1, keepdims=True) + EPSILON) * ROOT
    return values * scale, scale


def unit_pull(unit, scale, grad):
    return scale * (grad - unit * jnp.sum(unit * grad, axis=-1, keepdims=True))


def whole(count):
    return [pl.BlockSpec(memory_space=pltpu.VMEM)] * count


def call(kernel, out_shape, operands, scalars, flops, scratch=()):
    moved = sum(math.prod(a.shape) * a.dtype.itemsize for a in list(operands) + list(out_shape))
    return pl.pallas_call(
        kernel,
        out_shape=out_shape,
        in_specs=[pl.BlockSpec(memory_space=pltpu.SMEM)] * len(scalars) + whole(len(operands)),
        out_specs=whole(len(out_shape)),
        scratch_shapes=list(scratch),
        compiler_params=pltpu.CompilerParams(vmem_limit_bytes=VMEM_LIMIT),
        cost_estimate=pl.CostEstimate(flops=0, bytes_accessed=1, transcendentals=0),
    )(*scalars, *operands)


def prepare_kernel(feats, place, wide):
    row = lax.broadcasted_iota(jnp.int32, (ROWS, ROWS), 0)
    lane = lax.broadcasted_iota(jnp.int32, (ROWS, ROWS), 1)
    here = jnp.where(row == lane, place[...].astype(jnp.float32), 0.0)
    column = jnp.sum(here, axis=1, keepdims=True).astype(jnp.int32)
    digits = jnp.where(lane == 0, column // 128, jnp.where(lane == 1, column % 128, 0))
    wide[:, :D] = feats[...]
    wide[:, D:] = digits.astype(jnp.float32).astype(jnp.bfloat16)


def prepare(feats, place):
    return call(prepare_kernel, [bf16_shape(ROWS, WIDE)], [feats, place], [], 0)[0]


def bf16_shape(*shape):
    return jax.ShapeDtypeStruct(shape, jnp.bfloat16)


def f32_shape(*shape):
    return jax.ShapeDtypeStruct(shape, jnp.float32)


def text_unit_kernel(*refs):
    mine, near, far, out = refs[:STEPS], refs[STEPS], refs[STEPS + 1], refs[STEPS + 2]
    for n in range(2 * STEPS):
        other = near[...] if n < 2 else far[n // 2 - 1]
        raw = mine[n // 2][:, :D] if n % 2 == 0 else other
        out[n * ROWS : (n + 1) * ROWS, :] = unit_of(raw.astype(jnp.float32))[0].astype(jnp.bfloat16)


def side_kernel(*refs):
    for n, ref in enumerate(refs[:-1]):
        refs[-1][n] = ref[:, :D]


def side_by_side(pieces):
    return call(side_kernel, [bf16_shape(len(pieces), ROWS, D)], pieces, [], 0)[0]


def text_units(mine, other):
    return call(text_unit_kernel, [bf16_shape(2 * STEPS * ROWS, D)], [*mine, *other], [], 0)[0]


def rows_of(tiles):
    return sum(t.shape[0] for t in tiles)


def gather_feats(tiles):
    return jnp.concatenate([t[:, :D] for t in tiles], axis=0) if len(tiles) > 1 else tiles[0][:, :D]


def unit_kernel(count, weight, *refs):
    tiles, (low_ref, scale_ref, turned_ref, *first) = refs[:count], refs[count:]
    feats = gather_feats(tiles)
    unit, scale = unit_of(jnp.dot(feats, weight[...], preferred_element_type=jnp.float32))
    low_ref[...] = unit.astype(jnp.bfloat16)
    scale_ref[...] = jnp.broadcast_to(scale, scale_ref.shape)
    turned_ref[...] = feats.T
    for copy in first:
        copy[...] = tiles[0][:ROWS, :]


def image_units(weight, tiles, first=0):
    rows = rows_of(tiles)
    return call(
        functools.partial(unit_kernel, len(tiles)),
        [bf16_shape(rows, D), f32_shape(rows, 128), bf16_shape(D, rows)] + [bf16_shape(ROWS, WIDE)] * first,
        [weight, *tiles],
        [],
        2 * rows * D * D,
    )


def scalar_kernel(temper, offset_bias, loss_scale, out):
    row = lax.broadcasted_iota(jnp.int32, out.shape, 0)
    lower = jnp.where(row == 0, temper[0], offset_bias[0])
    out[...] = jnp.where(row < 2, lower, loss_scale[0] * temper[0])


def scalar_rows(temper, offset_bias, loss_scale):
    return call(scalar_kernel, [f32_shape(8, 128)], [], [temper, offset_bias, loss_scale], 0)[0]


def band(scalars, low, scale, place, texts, part_ref, grad_ref, turned_ref):
    temper, offset_bias, weighting = (scalars[n : n + 1, 0:1] for n in range(3))
    me = lax.axis_index("rep")
    mine = (me * ROWS).astype(jnp.float32)
    other = ((me + 1 - 2 * lax.rem(me, 2)) * ROWS).astype(jnp.float32)
    logits = (
        temper * lax.dot_general(low, texts[...], ROWS_BY_ROWS, preferred_element_type=jnp.float32)
        + offset_bias
    )
    lane = lax.broadcasted_iota(jnp.int32, (1, 2 * STEPS * ROWS), 1)
    spot = jnp.where(lane < 128, mine, other - 128.0) + lane.astype(jnp.float32)
    spot = jnp.where(lane < 256, spot, -1.0)
    match = place == spot
    sigmoid = 1.0 / (1.0 + jnp.exp(jnp.where(match, logits, -logits)))
    coeffs = (jnp.where(match, -weighting, weighting) * sigmoid).astype(jnp.bfloat16)
    turned_ref[...] = coeffs.T
    part = jnp.dot(coeffs, texts[...], preferred_element_type=jnp.float32)
    part_ref[...] = part.astype(jnp.bfloat16)
    unit = low.astype(jnp.float32)
    grad_ref[...] = unit_pull(unit, scale, part).astype(jnp.bfloat16)


def places(tiles):
    digits = [t[:, D:].astype(jnp.float32) for t in tiles]
    return jnp.concatenate([d[:, 0:1] * 128.0 + d[:, 1:2] for d in digits], axis=0)


def band_kernel(count, scalars, low, scale, texts, *refs):
    band(scalars, low[...], scale[:, 0:1], places(refs[:count]), texts, *refs[count:])


def band_shapes(rows):
    return [bf16_shape(rows, D), bf16_shape(rows, D), bf16_shape(2 * STEPS * ROWS, rows)]


def band_terms(scalars, low, scale, texts, tiles):
    rows = rows_of(tiles)
    return call(
        functools.partial(band_kernel, len(tiles)),
        band_shapes(rows),
        [scalars, low, scale, texts, *tiles],
        [],
        8 * rows * D * STEPS * ROWS,
    )


CUTS = ((0, 512), (512, 640))


def lay_out(lefts, rights, wide, deep):
    at = 0
    for left, right in zip(lefts, rights):
        rows = right.shape[0]
        wide[:, at : at + rows] = left[...]
        deep[at : at + rows, :] = right[...]
        at += rows


def slice_numbers():
    me = lax.axis_index("rep")
    core = lax.rem(me, 2)
    chip = (me - core) // 2
    way = 1 - 2 * core
    here, there = [me], [me + way]
    for k in (1, 2, 3, 4):
        below, above = lax.rem(chip - way * k + 8, 8), lax.rem(chip + way * k + 8, 8)
        here += [2 * below + core] + ([2 * below + 1 - core] if k < 4 else [])
        there += [2 * above + 1 - core] + ([2 * above + core] if k < 4 else [])
    return here, there


def head_kernel(count, *refs):
    feats, grads = refs[:count], refs[count : 2 * count]
    mine_ref, other_ref, wide, deep, total = refs[2 * count :]
    lay_out(feats, grads, wide, deep)
    for start, width in CUTS:
        total[:, start : start + width] = jnp.dot(
            wide[...], deep[:, start : start + width], preferred_element_type=jnp.float32
        )
    here, there = slice_numbers()
    for n in range(8):
        mine_ref[n] = total[pl.ds(pl.multiple_of(here[n] * SLICE, 8), SLICE), :].astype(jnp.bfloat16)
        other_ref[n] = total[pl.ds(pl.multiple_of(there[n] * SLICE, 8), SLICE), :].astype(jnp.bfloat16)


def head_terms(feats, grads):
    return call(
        functools.partial(head_kernel, len(feats)),
        [bf16_shape(8, SLICE, D), bf16_shape(8, SLICE, D)],
        [*feats, *grads],
        [],
        2 * 8 * ROWS * D * D,
        [
            pltpu.VMEM((D, 8 * ROWS), jnp.bfloat16),
            pltpu.VMEM((8 * ROWS, D), jnp.bfloat16),
            pltpu.VMEM((D, D), jnp.float32),
        ],
    )


def text_kernel(count, *refs):
    coeffs, units = refs[:count], refs[count : 2 * count]
    mine_ref, other_ref, wide, deep = refs[2 * count :]
    lay_out(coeffs, units, wide, deep)
    for start, width in CUTS:
        columns = slice(start, start + width)
        total = jnp.dot(wide[...], deep[:, columns], preferred_element_type=jnp.float32)
        for k in range(STEPS):
            mine_ref[k, :, columns] = total[2 * k * ROWS : (2 * k + 1) * ROWS]
            other_ref[k, :, columns] = total[(2 * k + 1) * ROWS : (2 * k + 2) * ROWS].astype(jnp.bfloat16)


def text_terms(coeffs, units):
    return call(
        functools.partial(text_kernel, len(coeffs)),
        [f32_shape(STEPS, ROWS, D), bf16_shape(STEPS, ROWS, D)],
        [*coeffs, *units],
        [],
        2 * 8 * ROWS * 2 * STEPS * ROWS * D,
        [pltpu.VMEM((2 * STEPS * ROWS, 8 * ROWS), jnp.bfloat16), pltpu.VMEM((8 * ROWS, D), jnp.bfloat16)],
    )


def text_sum_kernel(mine, other, own, one, two):
    own[...] = mine[0] + other[0].astype(jnp.float32)
    one[...] = (mine[1] + other[1].astype(jnp.float32)).astype(jnp.bfloat16)
    two[...] = (mine[2] + other[2].astype(jnp.float32)).astype(jnp.bfloat16)


def text_sums(mine, other):
    return call(
        text_sum_kernel, [f32_shape(ROWS, D), bf16_shape(ROWS, D), bf16_shape(ROWS, D)], [mine, other], [], 0
    )


def after(values, *others):
    return lax.optimization_barrier((values, others))[0]


def text_grad_kernel(raw, own, one, two, out):
    unit, scale = unit_of(raw[...].astype(jnp.float32))
    total = own[...] + one[...].astype(jnp.float32) + two[...].astype(jnp.float32)
    out[...] = unit_pull(unit, scale, total).astype(jnp.bfloat16)


def final_kernel(weight, low, scale, part, head, a_sum, b_sum, image_out, head_out):
    total = a_sum[...].astype(jnp.float32) + b_sum[...].astype(jnp.float32)
    grad = part[:ROWS, :].astype(jnp.float32) + total[:ROWS]
    unit = low[:ROWS, :].astype(jnp.float32)
    hidden_grad = unit_pull(unit, scale[:ROWS, 0:1], grad).astype(jnp.bfloat16)
    image_out[...] = lax.dot_general(
        hidden_grad, weight[...], ROWS_BY_ROWS, preferred_element_type=jnp.float32
    ).astype(jnp.bfloat16)
    head_out[0] = head[...] + total[ROWS:]


def ring_maps(chips):
    def dev(y, c):
        return 2 * (y % chips) + c

    out = [(dev(y, 0), dev(y + 1, 0)) for y in range(chips)] + [(dev(y, 1), dev(y - 1, 1)) for y in range(chips)]
    back = [(b, a) for a, b in out]
    out_two = [(dev(y, 0), dev(y + 2, 0)) for y in range(chips)] + [(dev(y, 1), dev(y - 2, 1)) for y in range(chips)]
    back_two = [(dev(y, 0), dev(y - 2, 0)) for y in range(chips)] + [(dev(y, 1), dev(y + 2, 1)) for y in range(chips)]
    cross = [(dev(y, 0), dev(y - 1, 1)) for y in range(chips)] + [(dev(y, 1), dev(y + 1, 0)) for y in range(chips)]
    swap = [(d, d ^ 1) for d in range(2 * chips)]
    return out, out_two, back, back_two, cross, swap


def shift(array, by):
    peers = lax.axis_size("blk")
    return lax.ppermute(array, "blk", [(i, (i + by) % peers) for i in range(peers)])


def local(image_feats, head_weight, text_embeds, positives, logit_scale, logit_bias, loss_scale):
    out, out_two, back, back_two, cross, swap = ring_maps(lax.axis_size("rep") // 2)
    f32, bf16 = jnp.float32, jnp.bfloat16

    def rep(array, pairs):
        return lax.ppermute(array, "rep", pairs)

    own = prepare(image_feats, positives)
    a_one, b_one = rep(own, out), rep(own, cross)
    text_one = shift(jnp.pad(text_embeds, ((0, 0), (0, 256))), 1)
    a_one, b_one, text_one = after((a_one, b_one, text_one))
    pair_one = jnp.concatenate([a_one, b_one], axis=0)
    pair_two = rep(pair_one, out)
    text_two = shift(text_one, 1)
    units = [image_units(head_weight, [own, pair_one])]
    scalars = scalar_rows(after(logit_scale, units[0]), logit_bias, loss_scale)
    near = rep(text_embeds, swap)
    pair_two = after(pair_two, units[0], scalars, near)
    pair_three = rep(pair_two, out)
    units.append(image_units(head_weight, [pair_two], 1))
    a_four = rep(units[1][3], out_two)
    text_two = after(text_two, units)
    far = rep(side_by_side([text_one, text_two]), swap)
    pair_three, far = after((pair_three, far))
    texts = text_units([text_embeds, text_one, text_two], [near, far])

    groups = [[own, pair_one], [pair_two], [pair_three], [a_four]]
    terms = [band_terms(scalars, u[0], u[1], texts, group) for u, group in zip(units, groups)]
    groups[2] = [after(pair_three, terms)]
    units.append(image_units(head_weight, groups[2]))
    terms.append(band_terms(scalars, units[2][0], units[2][1], texts, groups[2]))
    groups[3] = [after(a_four, terms)]
    units.append(image_units(head_weight, groups[3]))
    terms.append(band_terms(scalars, units[3][0], units[3][1], texts, groups[3]))
    part_groups = [t[0] for t in terms]
    parts = [p[n : n + ROWS] for p in part_groups for n in range(0, p.shape[0], ROWS)]

    head_mine, head_other = head_terms(
        [u[2] for u in units], [t[1] for t in terms]
    )
    head_sum = head_mine.astype(f32) + rep(head_other, swap).astype(f32)
    text_mine, text_other = text_terms(
        after([t[2] for t in terms], head_other), [u[0] for u in units]
    )

    def message(n, *came):
        total = jnp.concatenate([parts[n].astype(f32), head_sum[n]], axis=0)
        for other in came:
            total = total + other.astype(f32)
        return total.astype(bf16)

    a_sum, b_sum = rep(message(7), back), rep(message(6), back)
    a_next = message(5, a_sum)
    text_came = after(rep(text_other, swap), a_next)
    text_own, text_one_sum, text_two_sum = text_sums(text_mine, text_came)
    one_came, two_came = shift(text_one_sum, -1), shift(text_two_sum, -2)
    a_sum, b_sum = rep(a_next, back), rep(message(4, b_sum), back)
    a_sum, b_sum = rep(message(3, a_sum), back), rep(message(2, b_sum), cross)
    a_sum = after(a_sum, one_came, two_came)
    a_sum = rep(message(1, a_sum), back)
    image_grads, head_grad = call(
        final_kernel,
        [bf16_shape(ROWS, D), f32_shape(1, SLICE, D)],
        [head_weight, units[0][0], units[0][1], part_groups[0], head_sum[0], a_sum, b_sum],
        [],
        2 * ROWS * D * D,
    )
    (text_grads,) = call(
        text_grad_kernel,
        [bf16_shape(ROWS, D)],
        [text_embeds, text_own, one_came, two_came],
        [],
        0,
    )
    return (image_grads, text_grads, head_grad)


def solution(mesh):
    placed = (P(("blk", "rep"), None), P(), P(("blk", "rep"), None), P("blk", "rep"), P(), P(), P())
    return jax.shard_map(
        local,
        mesh=mesh,
        in_specs=placed,
        out_specs=(P(("blk", "rep"), None), P(("blk", "rep"), None), P("blk", "rep", None)),
        check_vma=False,
    )
```
